32 devices in a mesh: row: 8 (over z, core), col: 4 (over y, x).
Axes of the slice: x: 2, y: 2, z: 4, core: 2. Of those that a mesh axis runs over, the one named last changes fastest.
Arguments:
- front_blocks: bfloat16 [32, 5, 512, 512], P('row'), may hold values from -0.125 to 0.125
- block_cols: int32 [32, 5], P('row'), may hold values from 0 to 31, as said below
- samples: bfloat16 [16384, 1024], P('row', 'col'), may hold values from -6 to 6
- sketch_matrix: bfloat16 [1024, 256], replicated, may hold values from -0.1875 to 0.1875
Outputs:
- leaf_bases: bfloat16 [16384, 256], P('row')
- top_transfers: bfloat16 [1024, 256], P('row')
The draws below stay inside these ranges and needn't reach their ends.
Inputs may be any that keep to these rules, and one draw needn't show every extreme that they name: `block_cols`: each row lists 5 different block columns; the first is the row's own index, the second lies in the other half of the 32 block columns (its index differs in the highest bit).
All inputs are finite; a program needn't handle non-finite values.
Results may differ from the reference program's by a relative error of at most 0.035.
Values may be sent and summed in bfloat16 or wider, within the bound.
A program may use at most 128 MiB of HBM per device.

```python
import math
import jax
import jax.numpy as jnp
from jax import lax

LEAF = 512
RANK = 256
NS = 1024
K = 5
LEAVES = 32
ORDER = 16384
LEVELS = 5


def draw_block_cols(key, part):
    leaf_ids = jnp.arange(LEAVES, dtype=jnp.int32)
    cross_key = jax.random.fold_in(key, 11)
    crossing = LEAVES // 2 + jax.random.randint(cross_key, (LEAVES,), 0, LEAVES // 2, dtype=jnp.int32)
    row_keys = jax.random.split(jax.random.fold_in(key, 12), LEAVES)

    def near_masks(row_key):
        return jax.random.permutation(row_key, LEAVES // 2 - 1)[:K - 2].astype(jnp.int32) + 1
    nearby = jax.vmap(near_masks)(row_keys)
    xor_masks = jnp.concatenate([jnp.zeros((LEAVES, 1), jnp.int32), crossing[:, None], nearby], axis=1)
    return jnp.bitwise_xor(leaf_ids[:, None], xor_masks)


def level_of(rng, shape, shards, low, top_value):
    gain, own = 1.0, jax.random.fold_in(rng, 6)
    for dim, blocks in shards:
        heights = jnp.exp(jax.random.uniform(jax.random.fold_in(own, dim), (blocks,), jnp.float32, low / len(shards), top_value / len(shards)))
        gain = gain * jnp.repeat(heights, shape[dim] // blocks).reshape([-1 if axis == dim else 1 for axis in range(len(shape))])
    return gain


def centred(key, extent, scale, bound, cuts=(), kind=jnp.bfloat16):
    values = scale * jax.random.normal(key, extent, jnp.float32)
    if cuts:
        values = values * level_of(key, extent, cuts, -0.22, 0.18)
    return jnp.clip(values, -bound, bound).astype(kind)


def setup_inputs(seed: int = 0) -> dict:
    seeds = jax.random.split(jax.random.key(seed), 5)
    front_blocks = centred(seeds[0], (LEAVES, K, LEAF, LEAF), (K * LEAF) ** -0.5, 0.125, ((0, 8),))
    block_cols = draw_block_cols(jax.random.fold_in(seeds[4], 71), 0)
    samples = centred(seeds[2], (ORDER, NS), 1.0, 6.0, ((0, 8), (1, 4)))
    sketch_matrix = centred(seeds[3], (NS, RANK), NS ** -0.5, 0.1875)
    return {"front_blocks": front_blocks, "block_cols": block_cols, "samples": samples, "sketch_matrix": sketch_matrix}


def cholqr(sketch):
    highest = lax.Precision.HIGHEST
    gram_matrix = jnp.dot(sketch.T, sketch, precision=highest)
    low_factor = jnp.linalg.cholesky(gram_matrix)
    identity = jnp.eye(sketch.shape[1], dtype=sketch.dtype)
    low_inverse = jax.scipy.linalg.solve_triangular(low_factor, identity, lower=True)
    ortho_basis = jnp.dot(sketch, low_inverse.T, precision=highest)
    return (ortho_basis * math.sqrt(sketch.shape[0])).astype(jnp.bfloat16)

def reference(front_blocks, block_cols, samples, sketch_matrix):
    highest = lax.Precision.HIGHEST
    sketched = jnp.dot(samples.astype(jnp.float32), sketch_matrix.astype(jnp.float32), preferred_element_type=jnp.float32).astype(jnp.bfloat16)
    sample_blocks = sketched.reshape(LEAVES, LEAF, RANK)
    level_ids = jnp.arange(LEVELS, dtype=jnp.int32)

    def one_leaf(inputs):
        blocks, columns, leaf_id = inputs
        gathered_blocks = sample_blocks[columns].astype(jnp.float32)
        products = jnp.einsum('kab,kbc->kac', blocks.astype(jnp.float32), gathered_blocks, precision=highest)
        outside = (jnp.right_shift(leaf_id, level_ids)[:, None] != jnp.right_shift(columns[None, :], level_ids[:, None])).astype(jnp.float32)
        off_samples = jnp.einsum('lk,kac->lac', outside, products, precision=highest).astype(jnp.bfloat16)
        leaf_basis = cholqr(off_samples[0].astype(jnp.float32))
        projected = jnp.einsum('ar,lac->lrc', leaf_basis.astype(jnp.float32), off_samples[1:].astype(jnp.float32), precision=highest)
        projected = (projected * (1.0 / math.sqrt(LEAF))).astype(jnp.bfloat16)
        return (leaf_basis, projected)
    bases, projected = lax.map(one_leaf, (front_blocks, block_cols, jnp.arange(LEAVES, dtype=jnp.int32)))
    transfer = None
    for tree_level in range(1, LEVELS):
        node_count = projected.shape[0] // 2
        paired = projected.reshape(node_count, 2, projected.shape[1], RANK, RANK)
        stacked = jnp.concatenate([paired[:, 0], paired[:, 1]], axis=2)
        transfer = jax.vmap(cholqr)(stacked[:, 0].astype(jnp.float32))
        if tree_level < LEVELS - 1:
            moved = jnp.einsum('npr,nlpc->nlrc', transfer.astype(jnp.float32), stacked[:, 1:].astype(jnp.float32), precision=highest)
            projected = (moved * (1.0 / math.sqrt(2 * RANK))).astype(jnp.bfloat16)
    return (bases.reshape(LEAVES * LEAF, RANK), transfer.reshape(4 * RANK, RANK))
```

```python
import functools
import math

import jax
import jax.numpy as jnp
from jax import lax
from jax.experimental import pallas as pl
from jax.experimental.pallas import tpu as pltpu
from jax.sharding import PartitionSpec as P

PANEL = 32
STEP = 4
NT = (((1,), (1,)), ((), ()))
TN = (((0,), (0,)), ((), ()))


def swap(value, axis, mask):
    pairs = [(source, source ^ mask) for source in range(lax.axis_size(axis))]
    return lax.ppermute(value, axis, pairs)


def split3(value):
    high = value.astype(jnp.bfloat16)
    rest = value - high.astype(jnp.float32)
    mid = rest.astype(jnp.bfloat16)
    low = (rest - mid.astype(jnp.float32)).astype(jnp.bfloat16)
    return high, mid, low


def eliminate_panel(panel, start):
    rows, width = panel.shape
    row_ids = lax.broadcasted_iota(jnp.int32, (rows, 128), 0)
    wide_rows = lax.broadcasted_iota(jnp.int32, (rows, width), 0)
    lanes = lax.broadcasted_iota(jnp.int32, (rows, width), 1)
    pivots = jnp.ones((rows, 128), jnp.float32)
    for first in range(0, rows, STEP):
        cols = [
            jnp.broadcast_to(panel[:, start + first + t : start + first + t + 1], (rows, 128))
            for t in range(STEP)
        ]
        for t in range(STEP):
            j = first + t
            pivot = cols[t][j : j + 1, :]
            pivots = jnp.where(row_ids == j, pivot, pivots)
            factor = jnp.where(row_ids > j, cols[t] * (1.0 / pivot), 0.0)
            for u in range(t + 1, STEP):
                cols[u] = cols[u] - factor * cols[u][j : j + 1, :]
            panel = jnp.where(
                lanes == start + j, jnp.where(wide_rows == j, 1.0, 0.0), panel
            )
            panel = panel - jnp.concatenate([factor] * (width // 128), axis=1) * panel[j : j + 1, :]
    scale = lax.rsqrt(pivots)
    panel = panel * jnp.concatenate([scale] * (width // 128), axis=1)
    corner = (lanes > wide_rows + start) & (lanes < start + rows)
    return jnp.where(corner, 0.0, panel)


def cholqr_kernel(samples_ref, basis_ref, *rest):
    work_ref = rest[-1]
    rank = samples_ref.shape[1]
    count = samples_ref.shape[2]
    work_ref[...] = lax.dot_general(
        samples_ref[0], samples_ref[0], NT, preferred_element_type=jnp.float32
    )
    for start in range(0, rank, PANEL):
        end = start + PANEL
        panel = eliminate_panel(work_ref[start:end, :], start)
        work_ref[start:end, :] = panel
        if end < rank:
            update = lax.dot_general(
                panel, panel, TN, precision=lax.Precision.HIGHEST,
                preferred_element_type=jnp.float32,
            )
            later = work_ref[end:, :]
            lanes = lax.broadcasted_iota(jnp.int32, later.shape, 1)
            done = (lanes >= start) & (lanes < end)
            work_ref[end:, :] = jnp.where(done, 0.0, later) - update[end:, :]
    shape = (rank, rank)
    lower = lax.broadcasted_iota(jnp.int32, shape, 1) <= lax.broadcasted_iota(jnp.int32, shape, 0)
    inverse = jnp.where(lower, work_ref[...], 0.0)
    total = None
    for part in reversed(split3(inverse)):
        term = jnp.dot(part, samples_ref[0], preferred_element_type=jnp.float32)
        total = term if total is None else total + term
    basis = (total * math.sqrt(count)).astype(jnp.bfloat16)
    basis_ref[...] = basis
    if len(rest) > 1:
        moved_ref = rest[0]
        for level in range(moved_ref.shape[0]):
            moved = lax.dot_general(
                samples_ref[level + 1], basis, NT, preferred_element_type=jnp.float32
            )
            moved_ref[level] = (moved * (1.0 / math.sqrt(count))).astype(jnp.bfloat16)


def cholqr_project(samples):
    levels, rank, count = samples.shape
    out_shape = [jax.ShapeDtypeStruct((rank, count), jnp.bfloat16)]
    if levels > 1:
        out_shape.append(jax.ShapeDtypeStruct((levels - 1, rank, rank), jnp.bfloat16))
    vmem = pl.BlockSpec(memory_space=pltpu.VMEM)
    out = pl.pallas_call(
        cholqr_kernel,
        out_shape=out_shape,
        in_specs=[vmem],
        out_specs=[vmem] * len(out_shape),
        scratch_shapes=[pltpu.VMEM((rank, rank), jnp.float32)],
        compiler_params=pltpu.CompilerParams(vmem_limit_bytes=32 * 2**20),
    )(samples)
    return out if levels > 1 else (out[0], None)


def products_kernel(source_ref, depth_ref, blocks_ref, sketched_ref, out_ref):
    leaf = pl.program_id(0)
    slots = blocks_ref.shape[1]
    levels = out_ref.shape[1]
    sums = [jnp.zeros(out_ref.shape[2:], jnp.float32) for _ in range(levels)]
    for slot in range(slots):
        product = lax.dot_general(
            sketched_ref[source_ref[leaf, slot]], blocks_ref[0, slot], NT,
            preferred_element_type=jnp.float32,
        )
        depth = depth_ref[leaf, slot]
        for level in range(levels):
            sums[level] = sums[level] + jnp.where(depth > level, product, 0.0)
    for level in range(levels):
        out_ref[0, level] = sums[level].astype(jnp.bfloat16)


def off_products(front_blocks, sketched, source, depth, levels):
    leaf_dev, slots, size, _ = front_blocks.shape
    ranks = sketched.shape[1]
    grid_spec = pltpu.PrefetchScalarGridSpec(
        num_scalar_prefetch=2,
        grid=(leaf_dev,),
        in_specs=[
            pl.BlockSpec((1, slots, size, size), lambda i, *_: (i, 0, 0, 0)),
            pl.BlockSpec(sketched.shape, lambda i, *_: (0, 0, 0)),
        ],
        out_specs=pl.BlockSpec((1, levels, ranks, size), lambda i, *_: (i, 0, 0, 0)),
    )
    return pl.pallas_call(
        products_kernel,
        grid_spec=grid_spec,
        out_shape=jax.ShapeDtypeStruct((leaf_dev, levels, ranks, size), jnp.bfloat16),
        compiler_params=pltpu.CompilerParams(vmem_limit_bytes=40 * 2**20),
    )(source, depth, front_blocks, sketched)


def shards(front_blocks, block_cols, samples, sketch_matrix):
    leaf_dev, _, leaf_size, _ = front_blocks.shape
    rank = sketch_matrix.shape[1]
    cols_dev = samples.shape[1]
    size_rows, size_cols = lax.axis_size("row"), lax.axis_size("col")
    row, col = lax.axis_index("row"), lax.axis_index("col")
    leaf_total = leaf_dev * size_rows
    top_level = leaf_total.bit_length() - 1
    local_levels = leaf_dev.bit_length() - 1
    chunk = rank // size_cols

    local_rows = lax.dynamic_slice_in_dim(sketch_matrix, col * cols_dev, cols_dev, 0)
    partial = jnp.einsum(
        "kc,lak->lca",
        local_rows,
        samples.reshape(leaf_dev, leaf_size, cols_dev),
        preferred_element_type=jnp.float32,
    ).astype(jnp.bfloat16)

    def chunk_of(owner):
        return lax.dynamic_slice_in_dim(partial, owner * chunk, chunk, 1)

    received = [swap(chunk_of(col ^ mask), "col", mask) for mask in range(1, size_cols)]
    total = chunk_of(col).astype(jnp.float32)
    for term in received:
        total = total + term.astype(jnp.float32)
    sketched = total.astype(jnp.bfloat16)

    even = jnp.stack([sketched] + [swap(sketched, "row", mask) for mask in range(2, size_rows, 2)])
    odd = swap(even, "row", 1)
    held = jnp.concatenate([even, odd]).reshape(leaf_total, chunk, leaf_size)
    leaf_ids = row * leaf_dev + jnp.arange(leaf_dev, dtype=jnp.int32)
    apart = jnp.bitwise_xor(leaf_ids[:, None], block_cols)
    depth = sum((apart >> level > 0).astype(jnp.int32) for level in range(top_level))
    offset = (block_cols // leaf_dev) ^ row
    place = (offset & 1) * (size_rows // 2) + (offset >> 1)
    source = place * leaf_dev + block_cols % leaf_dev

    off = off_products(front_blocks, held, source, depth, top_level)

    def leaf_of(owner):
        return lax.dynamic_index_in_dim(off, owner % leaf_dev, 0, keepdims=False)

    pieces = jnp.stack(
        [leaf_of(col)] + [swap(leaf_of(col ^ mask), "col", mask) for mask in range(1, size_cols)]
    )
    ordered = pieces[jnp.arange(size_cols, dtype=jnp.int32) ^ col]
    stacked = ordered.swapaxes(0, 1).reshape(top_level, rank, leaf_size)

    basis, carried = cholqr_project(stacked)
    own = basis.T
    bases = jnp.stack([own] + [swap(own, "col", mask) for mask in range(1, leaf_dev)])
    bases = bases[jnp.arange(leaf_dev, dtype=jnp.int32) ^ (col % leaf_dev)]

    for tree_level in range(1, top_level):
        bit = tree_level - 1
        if bit < local_levels:
            axis, index = "col", col
        else:
            axis, index, bit = "row", row, bit - local_levels
        is_left = (index >> bit) % 2 == 0
        partner = swap(carried, axis, 2**bit)
        stacked = jnp.concatenate(
            [jnp.where(is_left, carried, partner), jnp.where(is_left, partner, carried)], axis=2
        )
        transfer, carried = cholqr_project(stacked)
    out_rows = 4 * rank // size_rows
    offset = row % (size_rows // 2) * out_rows
    top_rows = lax.dynamic_slice_in_dim(transfer.T, offset, out_rows, 0)
    return (bases.reshape(leaf_dev * leaf_size, rank), top_rows)


def solution(mesh):
    placed = (P("row", None, None, None), P("row", None), P("row", "col"), P())
    return jax.shard_map(
        shards,
        mesh=mesh,
        in_specs=placed,
        out_specs=(P("row", None), P("row", None)),
        check_vma=False,
    )
```

```python
import functools
import math

import jax
import jax.numpy as jnp
from jax import lax
from jax.experimental import pallas as pl
from jax.experimental.pallas import tpu as pltpu
from jax.sharding import PartitionSpec as P

PANEL = 32
BUSY = 8 * 10**9
NT = (((1,), (1,)), ((), ()))
TN = (((0,), (0,)), ((), ()))


def swap(value, axis, mask):
    pairs = [(source, source ^ mask) for source in range(lax.axis_size(axis))]
    return lax.ppermute(value, axis, pairs)


def split3(value):
    high = value.astype(jnp.bfloat16)
    rest = value - high.astype(jnp.float32)
    mid = rest.astype(jnp.bfloat16)
    low = (rest - mid.astype(jnp.float32)).astype(jnp.bfloat16)
    return high, mid, low


def reciprocal(value):
    guess = pl.reciprocal(value, approx=True)
    return guess * (2.0 - value * guess)


def wide(value, width):
    return jnp.concatenate([value] * (width // value.shape[1]), axis=1)


def eliminate_panel(panel, start):
    rows, width = panel.shape
    tiles = [panel[8 * i : 8 * i + 8, :] for i in range(rows // 8)]
    lanes = lax.broadcasted_iota(jnp.int32, (8, width), 1)
    row_ids = lax.broadcasted_iota(jnp.int32, (8, width), 0)
    for k in range(len(tiles)):
        base = start + 8 * k
        inside = (lanes >= base) & (lanes < base + 8)
        unit = jnp.where(lanes == base + row_ids, 1.0, 0.0)

        def columns(tile):
            return [
                jnp.broadcast_to(tile[:, base + t : base + t + 1], (8, 128)) for t in range(8)
            ]

        below = {i: columns(tiles[i]) for i in range(k + 1, len(tiles))}
        own = columns(tiles[k])
        values = [
            [jnp.broadcast_to(own[u][t : t + 1, :], (8, 128)) if u >= t else None for u in range(8)]
            for t in range(8)
        ]
        top = jnp.where(inside, unit, tiles[k])
        lines = [jnp.broadcast_to(top[t : t + 1, :], (8, width)) for t in range(8)]
        inverses, new = [], None
        for t in range(8):
            inverse = reciprocal(values[t][t])
            inverses.append(inverse)
            for u in range(t + 1, 8):
                ratio = values[t][u] * inverse
                for v in range(u, 8):
                    values[u][v] = values[u][v] - ratio * values[t][v]
                lines[u] = lines[u] - wide(ratio, width) * lines[t]
            scaled = lines[t] * wide(lax.rsqrt(values[t][t]), width)
            new = scaled if new is None else jnp.where(row_ids == t, scaled, new)
        for i in range(len(tiles)):
            if i == k:
                tiles[i] = new
                continue
            tile = jnp.where(inside, 0.0, tiles[i])
            if i > k:
                cols = below[i]
                for t in range(8):
                    factor = cols[t] * inverses[t]
                    for u in range(t + 1, 8):
                        cols[u] = cols[u] - factor * values[t][u]
                    tile = tile - wide(factor, width) * lines[t]
            tiles[i] = tile
    return jnp.concatenate(tiles, axis=0)


def invert_factor(work_ref):
    rank = work_ref.shape[0]
    for start in range(0, rank, PANEL):
        end = start + PANEL
        panel = eliminate_panel(work_ref[start:end, :], start)
        work_ref[start:end, :] = panel
        if end < rank:
            high, mid, low = split3(panel)
            left = jnp.concatenate([high, high, mid, high, low, mid], axis=0)
            right = jnp.concatenate([high, mid, high, low, high, mid], axis=0)
            first = end // 128 * 128
            update = lax.dot_general(
                left[:, first:], right, TN, preferred_element_type=jnp.float32
            )
            later = work_ref[end:, :]
            lanes = lax.broadcasted_iota(jnp.int32, later.shape, 1)
            done = (lanes >= start) & (lanes < end)
            work_ref[end:, :] = jnp.where(done, 0.0, later) - update[end - first :, :]
    shape = (rank, rank)
    lower = lax.broadcasted_iota(jnp.int32, shape, 1) <= lax.broadcasted_iota(jnp.int32, shape, 0)
    return split3(jnp.where(lower, work_ref[...], 0.0))


def gram(value):
    return lax.dot_general(value, value, NT, preferred_element_type=jnp.float32)


def apply_inverse(parts, value, count):
    total = None
    for part in reversed(parts):
        term = jnp.dot(part, value, preferred_element_type=jnp.float32)
        total = term if total is None else total + term
    return (total * math.sqrt(count)).astype(jnp.bfloat16)


def leaf_kernel(col_ref, *refs):
    pieces, (basis_ref, rows_ref, samples_ref, work_ref) = refs[:-4], refs[-4:]
    chunk, count = pieces[0].shape
    for mask, piece in enumerate(pieces):
        place = pl.multiple_of((col_ref[0] ^ mask) * chunk, chunk)
        samples_ref[pl.ds(place, chunk), :] = piece[...]
    work_ref[...] = gram(samples_ref[...])
    parts = invert_factor(work_ref)
    basis = apply_inverse(parts, samples_ref[...], count)
    basis_ref[...] = basis
    rows_ref[...] = basis.T


def node_kernel(own_ref, partner_ref, *refs):
    outs, work_ref = refs[:-1], refs[-1]
    count = 2 * own_ref.shape[1]
    work_ref[...] = gram(own_ref[...]) + gram(partner_ref[...])
    parts = invert_factor(work_ref)
    for source, out in zip((own_ref, partner_ref), outs):
        out[...] = apply_inverse(parts, source[...], count)


def project_leaf_kernel(col_ref, basis_ref, *refs):
    pieces, (first_ref, rest_ref) = refs[:-2], refs[-2:]
    levels, chunk, count = pieces[0].shape
    for mask, piece in enumerate(pieces):
        place = pl.ds(pl.multiple_of((col_ref[0] ^ mask) * chunk, chunk), chunk)
        for level in range(levels):
            moved = lax.dot_general(
                piece[level], basis_ref[...], NT, preferred_element_type=jnp.float32
            )
            moved = (moved * (1.0 / math.sqrt(count))).astype(jnp.bfloat16)
            if level:
                rest_ref[level - 1, place, :] = moved
            else:
                first_ref[place, :] = moved


def project_node_kernel(own_ref, partner_ref, q_own_ref, q_partner_ref, first_ref, *rest):
    count = 2 * own_ref.shape[2]
    for level in range(own_ref.shape[0]):
        moved = lax.dot_general(
            own_ref[level], q_own_ref[...], NT, preferred_element_type=jnp.float32
        ) + lax.dot_general(
            partner_ref[level], q_partner_ref[...], NT, preferred_element_type=jnp.float32
        )
        moved = (moved * (1.0 / math.sqrt(count))).astype(jnp.bfloat16)
        if level:
            rest[0][level - 1] = moved
        else:
            first_ref[...] = moved


def local_call(kernel, args, shapes, scalars=0, scratch=(), flops=0):
    vmem = pl.BlockSpec(memory_space=pltpu.VMEM)
    smem = pl.BlockSpec(memory_space=pltpu.SMEM)
    return pl.pallas_call(
        kernel,
        out_shape=[jax.ShapeDtypeStruct(shape, jnp.bfloat16) for shape in shapes],
        in_specs=[smem] * scalars + [vmem] * (len(args) - scalars),
        out_specs=[vmem] * len(shapes),
        scratch_shapes=list(scratch),
        cost_estimate=pl.CostEstimate(flops=flops, bytes_accessed=2**20, transcendentals=0),
        compiler_params=pltpu.CompilerParams(vmem_limit_bytes=32 * 2**20),
    )(*args)


def products_kernel(source_ref, depth_ref, blocks_ref, sketched_ref, first_ref, rest_ref):
    leaf = pl.program_id(0)
    slots = blocks_ref.shape[1]
    levels = rest_ref.shape[1] + 1
    sums = [jnp.zeros(first_ref.shape[1:], jnp.float32) for _ in range(levels)]
    for slot in range(slots):
        product = lax.dot_general(
            sketched_ref[source_ref[leaf, slot]], blocks_ref[0, slot], NT,
            preferred_element_type=jnp.float32,
        )
        depth = depth_ref[leaf, slot]
        for level in range(levels):
            sums[level] = sums[level] + jnp.where(depth > level, product, 0.0)
    first_ref[0] = sums[0].astype(jnp.bfloat16)
    for level in range(1, levels):
        rest_ref[0, level - 1] = sums[level].astype(jnp.bfloat16)


def off_products(front_blocks, sketched, source, depth, levels):
    leaf_dev, slots, size, _ = front_blocks.shape
    ranks = sketched.shape[1]
    grid_spec = pltpu.PrefetchScalarGridSpec(
        num_scalar_prefetch=2,
        grid=(leaf_dev,),
        in_specs=[
            pl.BlockSpec((1, slots, size, size), lambda i, *_: (i, 0, 0, 0)),
            pl.BlockSpec(sketched.shape, lambda i, *_: (0, 0, 0)),
        ],
        out_specs=[
            pl.BlockSpec((1, ranks, size), lambda i, *_: (i, 0, 0)),
            pl.BlockSpec((1, levels - 1, ranks, size), lambda i, *_: (i, 0, 0, 0)),
        ],
    )
    return pl.pallas_call(
        products_kernel,
        grid_spec=grid_spec,
        out_shape=[
            jax.ShapeDtypeStruct((leaf_dev, ranks, size), jnp.bfloat16),
            jax.ShapeDtypeStruct((leaf_dev, levels - 1, ranks, size), jnp.bfloat16),
        ],
        compiler_params=pltpu.CompilerParams(vmem_limit_bytes=40 * 2**20),
    )(source, depth, front_blocks, sketched)


def shards(front_blocks, block_cols, samples, sketch_matrix):
    leaf_dev, _, leaf_size, _ = front_blocks.shape
    rank = sketch_matrix.shape[1]
    cols_dev = samples.shape[1]
    size_rows, size_cols = lax.axis_size("row"), lax.axis_size("col")
    row, col = lax.axis_index("row"), lax.axis_index("col")
    leaf_total = leaf_dev * size_rows
    top_level = leaf_total.bit_length() - 1
    local_levels = leaf_dev.bit_length() - 1
    chunk = rank // size_cols

    local_rows = lax.dynamic_slice_in_dim(sketch_matrix, col * cols_dev, cols_dev, 0)
    partial = jnp.einsum(
        "kc,lak->lca",
        local_rows,
        samples.reshape(leaf_dev, leaf_size, cols_dev),
        preferred_element_type=jnp.float32,
    ).astype(jnp.bfloat16)

    def chunk_of(owner):
        return lax.dynamic_slice_in_dim(partial, owner * chunk, chunk, 1)

    received = [swap(chunk_of(col ^ mask), "col", mask) for mask in range(1, size_cols)]
    total = chunk_of(col).astype(jnp.float32)
    for term in received:
        total = total + term.astype(jnp.float32)
    sketched = total.astype(jnp.bfloat16)

    even = jnp.stack([sketched] + [swap(sketched, "row", mask) for mask in range(2, size_rows, 2)])
    odd = swap(even, "row", 1)
    held = jnp.concatenate([even, odd]).reshape(leaf_total, chunk, leaf_size)
    leaf_ids = row * leaf_dev + jnp.arange(leaf_dev, dtype=jnp.int32)
    apart = jnp.bitwise_xor(leaf_ids[:, None], block_cols)
    depth = sum((apart >> level > 0).astype(jnp.int32) for level in range(top_level))
    offset = (block_cols // leaf_dev) ^ row
    place = (offset & 1) * (size_rows // 2) + (offset >> 1)
    source = place * leaf_dev + block_cols % leaf_dev

    off_first, off_rest = off_products(front_blocks, held, source, depth, top_level)

    def leaf_of(off, mask):
        return lax.dynamic_index_in_dim(off, (col ^ mask) % leaf_dev, 0, keepdims=False)

    masks = range(1, size_cols)
    here = col.astype(jnp.int32).reshape(1)
    pieces = [leaf_of(off_first, 0)] + [swap(leaf_of(off_first, m), "col", m) for m in masks]
    pieces, off_rest = lax.optimization_barrier((pieces, off_rest))
    later = [leaf_of(off_rest, 0)] + [swap(leaf_of(off_rest, m), "col", m) for m in masks]
    work = pltpu.VMEM((rank, rank), jnp.float32)
    basis, basis_rows = local_call(
        leaf_kernel, [here, *pieces], [(rank, leaf_size), (leaf_size, rank)], 1,
        [pltpu.VMEM((rank, leaf_size), jnp.bfloat16), work], BUSY,
    )
    first, rest = local_call(
        project_leaf_kernel, [here, basis, *later],
        [(rank, rank), (top_level - 2, rank, rank)], 1,
    )

    square = (rank, rank)
    bases = None
    for tree_level in range(1, top_level):
        bit = tree_level - 1
        axis = "col" if bit < local_levels else "row"
        mask = 2 ** (bit if axis == "col" else bit - local_levels)
        partner = swap(first, axis, mask)
        if tree_level == top_level - 1:
            (transfer,) = local_call(node_kernel, [first, partner], [square], 0, [work], BUSY)
            break
        partner, rest = lax.optimization_barrier((partner, rest))
        partner_rest = swap(rest, axis, mask)
        if axis == "row" and bases is None:
            partner, basis_rows = lax.optimization_barrier((partner, basis_rows))
            groups = [
                list(range(i, i + leaf_dev)) for i in range(0, size_cols, leaf_dev)
            ]
            bases = lax.all_gather(
                basis_rows, "col", axis=0, tiled=True, axis_index_groups=groups
            )
        q_own, q_partner = local_call(
            node_kernel, [first, partner], [square, square], 0, [work], BUSY
        )
        shapes = [square] + [(rest.shape[0] - 1, *square)] * (rest.shape[0] > 1)
        first, *others = local_call(
            project_node_kernel, [rest, partner_rest, q_own, q_partner], shapes
        )
        rest = others[0] if others else None
    out_rows = 4 * rank // size_rows
    top_rows = lax.dynamic_slice_in_dim(transfer, row * out_rows % rank, out_rows, 1).T
    return (bases, top_rows)


def solution(mesh):
    placed = (P("row", None, None, None), P("row", None), P("row", "col"), P())
    return jax.shard_map(
        shards,
        mesh=mesh,
        in_specs=placed,
        out_specs=(P("row", None), P("row", None)),
        check_vma=False,
    )
```

```python
import functools
import math

import jax
import jax.numpy as jnp
from jax import lax
from jax.experimental import pallas as pl
from jax.experimental.pallas import tpu as pltpu
from jax.sharding import PartitionSpec as P

PANEL = 32
BUSY = 8 * 10**9
NT = (((1,), (1,)), ((), ()))
TN = (((0,), (0,)), ((), ()))


def swap(value, axis, mask):
    pairs = [(source, source ^ mask) for source in range(lax.axis_size(axis))]
    return lax.ppermute(value, axis, pairs)


def split3(value):
    high = value.astype(jnp.bfloat16)
    rest = value - high.astype(jnp.float32)
    mid = rest.astype(jnp.bfloat16)
    low = (rest - mid.astype(jnp.float32)).astype(jnp.bfloat16)
    return high, mid, low


def reciprocal(value):
    guess = pl.reciprocal(value, approx=True)
    return guess * (2.0 - value * guess)


def wide(value, width):
    return jnp.concatenate([value] * (width // value.shape[1]), axis=1)


def eliminate_panel(panel, start):
    rows, width = panel.shape
    tiles = [panel[8 * i : 8 * i + 8, :] for i in range(rows // 8)]
    lanes = lax.broadcasted_iota(jnp.int32, (8, width), 1)
    row_ids = lax.broadcasted_iota(jnp.int32, (8, width), 0)
    for k in range(len(tiles)):
        base = start + 8 * k
        inside = (lanes >= base) & (lanes < base + 8)
        unit = jnp.where(lanes == base + row_ids, 1.0, 0.0)

        def columns(tile):
            return [
                jnp.broadcast_to(tile[:, base + t : base + t + 1], (8, 128)) for t in range(8)
            ]

        below = {i: columns(tiles[i]) for i in range(k + 1, len(tiles))}
        own = columns(tiles[k])
        values = [
            [jnp.broadcast_to(own[u][t : t + 1, :], (8, 128)) if u >= t else None for u in range(8)]
            for t in range(8)
        ]
        top = jnp.where(inside, unit, tiles[k])
        lines = [jnp.broadcast_to(top[t : t + 1, :], (8, width)) for t in range(8)]
        inverses, new = [], None
        for t in range(8):
            inverse = reciprocal(values[t][t])
            inverses.append(inverse)
            for u in range(t + 1, 8):
                ratio = values[t][u] * inverse
                for v in range(u, 8):
                    values[u][v] = values[u][v] - ratio * values[t][v]
                lines[u] = lines[u] - wide(ratio, width) * lines[t]
            scaled = lines[t] * wide(lax.rsqrt(values[t][t]), width)
            new = scaled if new is None else jnp.where(row_ids == t, scaled, new)
        for i in range(len(tiles)):
            if i == k:
                tiles[i] = new
                continue
            tile = jnp.where(inside, 0.0, tiles[i])
            if i > k:
                cols = below[i]
                for t in range(8):
                    factor = cols[t] * inverses[t]
                    for u in range(t + 1, 8):
                        cols[u] = cols[u] - factor * values[t][u]
                    tile = tile - wide(factor, width) * lines[t]
            tiles[i] = tile
    return jnp.concatenate(tiles, axis=0)


def invert_factor(work_ref):
    rank = work_ref.shape[0]
    for start in range(0, rank, PANEL):
        end = start + PANEL
        panel = eliminate_panel(work_ref[start:end, :], start)
        work_ref[start:end, :] = panel
        if end < rank:
            high, mid, low = split3(panel)
            left = jnp.concatenate([high, high, mid, high, low, mid], axis=0)
            right = jnp.concatenate([high, mid, high, low, high, mid], axis=0)
            first = end // 128 * 128
            update = lax.dot_general(
                left[:, first:], right, TN, preferred_element_type=jnp.float32
            )
            later = work_ref[end:, :]
            lanes = lax.broadcasted_iota(jnp.int32, later.shape, 1)
            done = (lanes >= start) & (lanes < end)
            work_ref[end:, :] = jnp.where(done, 0.0, later) - update[end - first :, :]
    shape = (rank, rank)
    lower = lax.broadcasted_iota(jnp.int32, shape, 1) <= lax.broadcasted_iota(jnp.int32, shape, 0)
    return split3(jnp.where(lower, work_ref[...], 0.0))


def gram(value):
    return lax.dot_general(value, value, NT, preferred_element_type=jnp.float32)


def apply_inverse(parts, value, count):
    total = None
    for part in reversed(parts):
        term = jnp.dot(part, value, preferred_element_type=jnp.float32)
        total = term if total is None else total + term
    return (total * math.sqrt(count)).astype(jnp.bfloat16)


def leaf_kernel(col_ref, *refs):
    pieces, (basis_ref, rows_ref, samples_ref, work_ref) = refs[:-4], refs[-4:]
    chunk, count = pieces[0].shape
    for mask, piece in enumerate(pieces):
        place = pl.multiple_of((col_ref[0] ^ mask) * chunk, chunk)
        samples_ref[pl.ds(place, chunk), :] = piece[...]
    work_ref[...] = gram(samples_ref[...])
    parts = invert_factor(work_ref)
    basis = apply_inverse(parts, samples_ref[...], count)
    basis_ref[...] = basis
    rows_ref[...] = basis.T


def node_kernel(own_ref, partner_ref, *refs):
    outs, work_ref = refs[:-1], refs[-1]
    count = 2 * own_ref.shape[1]
    work_ref[...] = gram(own_ref[...]) + gram(partner_ref[...])
    parts = invert_factor(work_ref)
    for source, out in zip((own_ref, partner_ref), outs):
        out[...] = apply_inverse(parts, source[...], count)


def project_leaf_kernel(col_ref, basis_ref, *refs):
    pieces, (first_ref, rest_ref) = refs[:-2], refs[-2:]
    levels, chunk, count = pieces[0].shape
    for mask, piece in enumerate(pieces):
        place = pl.ds(pl.multiple_of((col_ref[0] ^ mask) * chunk, chunk), chunk)
        for level in range(levels):
            moved = lax.dot_general(
                piece[level], basis_ref[...], NT, preferred_element_type=jnp.float32
            )
            moved = (moved * (1.0 / math.sqrt(count))).astype(jnp.bfloat16)
            if level:
                rest_ref[level - 1, place, :] = moved
            else:
                first_ref[place, :] = moved


def project_node_kernel(own_ref, partner_ref, q_own_ref, q_partner_ref, first_ref, *rest):
    count = 2 * own_ref.shape[2]
    for level in range(own_ref.shape[0]):
        moved = lax.dot_general(
            own_ref[level], q_own_ref[...], NT, preferred_element_type=jnp.float32
        ) + lax.dot_general(
            partner_ref[level], q_partner_ref[...], NT, preferred_element_type=jnp.float32
        )
        moved = (moved * (1.0 / math.sqrt(count))).astype(jnp.bfloat16)
        if level:
            rest[0][level - 1] = moved
        else:
            first_ref[...] = moved


def local_call(kernel, args, shapes, scalars=0, scratch=(), flops=0):
    vmem = pl.BlockSpec(memory_space=pltpu.VMEM)
    smem = pl.BlockSpec(memory_space=pltpu.SMEM)
    return pl.pallas_call(
        kernel,
        out_shape=[jax.ShapeDtypeStruct(shape, jnp.bfloat16) for shape in shapes],
        in_specs=[smem] * scalars + [vmem] * (len(args) - scalars),
        out_specs=[vmem] * len(shapes),
        scratch_shapes=list(scratch),
        cost_estimate=pl.CostEstimate(flops=flops, bytes_accessed=2**20, transcendentals=0),
        compiler_params=pltpu.CompilerParams(vmem_limit_bytes=32 * 2**20),
    )(*args)


def products_kernel(source_ref, depth_ref, blocks_ref, sketched_ref, first_ref, rest_ref):
    leaf = pl.program_id(0)
    slots = blocks_ref.shape[1]
    levels = rest_ref.shape[1] + 1
    sums = [jnp.zeros(first_ref.shape[1:], jnp.float32) for _ in range(levels)]
    for slot in range(slots):
        product = lax.dot_general(
            sketched_ref[source_ref[leaf, slot]], blocks_ref[0, slot], NT,
            preferred_element_type=jnp.float32,
        )
        depth = depth_ref[leaf, slot]
        for level in range(levels):
            sums[level] = sums[level] + jnp.where(depth > level, product, 0.0)
    first_ref[0] = sums[0].astype(jnp.bfloat16)
    for level in range(1, levels):
        rest_ref[0, level - 1] = sums[level].astype(jnp.bfloat16)


def off_products(front_blocks, sketched, source, depth, levels):
    leaf_dev, slots, size, _ = front_blocks.shape
    ranks = sketched.shape[1]
    grid_spec = pltpu.PrefetchScalarGridSpec(
        num_scalar_prefetch=2,
        grid=(leaf_dev,),
        in_specs=[
            pl.BlockSpec((1, slots, size, size), lambda i, *_: (i, 0, 0, 0)),
            pl.BlockSpec(sketched.shape, lambda i, *_: (0, 0, 0)),
        ],
        out_specs=[
            pl.BlockSpec((1, ranks, size), lambda i, *_: (i, 0, 0)),
            pl.BlockSpec((1, levels - 1, ranks, size), lambda i, *_: (i, 0, 0, 0)),
        ],
    )
    return pl.pallas_call(
        products_kernel,
        grid_spec=grid_spec,
        out_shape=[
            jax.ShapeDtypeStruct((leaf_dev, ranks, size), jnp.bfloat16),
            jax.ShapeDtypeStruct((leaf_dev, levels - 1, ranks, size), jnp.bfloat16),
        ],
        compiler_params=pltpu.CompilerParams(vmem_limit_bytes=40 * 2**20),
    )(source, depth, front_blocks, sketched)


def shards(front_blocks, block_cols, samples, sketch_matrix):
    leaf_dev, _, leaf_size, _ = front_blocks.shape
    rank = sketch_matrix.shape[1]
    cols_dev = samples.shape[1]
    size_rows, size_cols = lax.axis_size("row"), lax.axis_size("col")
    row, col = lax.axis_index("row"), lax.axis_index("col")
    leaf_total = leaf_dev * size_rows
    top_level = leaf_total.bit_length() - 1
    local_levels = leaf_dev.bit_length() - 1
    chunk = rank // size_cols

    local_rows = lax.dynamic_slice_in_dim(sketch_matrix, col * cols_dev, cols_dev, 0)
    partial = jnp.einsum(
        "kc,lak->lca",
        local_rows,
        samples.reshape(leaf_dev, leaf_size, cols_dev),
        preferred_element_type=jnp.float32,
    ).astype(jnp.bfloat16)

    def chunk_of(owner):
        return lax.dynamic_slice_in_dim(partial, owner * chunk, chunk, 1)

    received = [swap(chunk_of(col ^ mask), "col", mask) for mask in range(1, size_cols)]
    total = chunk_of(col).astype(jnp.float32)
    for term in received:
        total = total + term.astype(jnp.float32)
    sketched = total.astype(jnp.bfloat16)

    even = jnp.stack([sketched] + [swap(sketched, "row", mask) for mask in range(2, size_rows, 2)])
    odd = swap(even, "row", 1)
    held = jnp.concatenate([even, odd]).reshape(leaf_total, chunk, leaf_size)
    leaf_ids = row * leaf_dev + jnp.arange(leaf_dev, dtype=jnp.int32)
    apart = jnp.bitwise_xor(leaf_ids[:, None], block_cols)
    depth = sum((apart >> level > 0).astype(jnp.int32) for level in range(top_level))
    offset = (block_cols // leaf_dev) ^ row
    place = (offset & 1) * (size_rows // 2) + (offset >> 1)
    source = place * leaf_dev + block_cols % leaf_dev

    off_first, off_rest = off_products(front_blocks, held, source, depth, top_level)

    def leaf_of(off, mask):
        return lax.dynamic_index_in_dim(off, (col ^ mask) % leaf_dev, 0, keepdims=False)

    masks = range(1, size_cols)
    here = col.astype(jnp.int32).reshape(1)
    pieces = [leaf_of(off_first, 0)] + [swap(leaf_of(off_first, m), "col", m) for m in masks]
    pieces, off_rest = lax.optimization_barrier((pieces, off_rest))
    later = [leaf_of(off_rest, 0)] + [swap(leaf_of(off_rest, m), "col", m) for m in masks]
    work = pltpu.VMEM((rank, rank), jnp.float32)
    basis, basis_rows = local_call(
        leaf_kernel, [here, *pieces], [(rank, leaf_size), (leaf_size, rank)], 1,
        [pltpu.VMEM((rank, leaf_size), jnp.bfloat16), work], BUSY,
    )
    first, rest = local_call(
        project_leaf_kernel, [here, basis, *later],
        [(rank, rank), (top_level - 2, rank, rank)], 1,
    )

    square = (rank, rank)
    bases = None
    for tree_level in range(1, top_level):
        bit = tree_level - 1
        axis = "col" if bit < local_levels else "row"
        mask = 2 ** (bit if axis == "col" else bit - local_levels)
        partner = swap(first, axis, mask)
        if tree_level == top_level - 1:
            (transfer,) = local_call(node_kernel, [first, partner], [square], 0, [work], BUSY)
            break
        partner, rest = lax.optimization_barrier((partner, rest))
        partner_rest = swap(rest, axis, mask)
        if axis == "row" and bases is None:
            partner, basis_rows = lax.optimization_barrier((partner, basis_rows))
            bases = [basis_rows] + [swap(basis_rows, "col", m) for m in range(1, leaf_dev)]
            order = jnp.arange(leaf_dev, dtype=jnp.int32) ^ (col % leaf_dev)
            bases = jnp.stack(bases)[order].reshape(leaf_dev * leaf_size, rank)
        q_own, q_partner = local_call(
            node_kernel, [first, partner], [square, square], 0, [work], BUSY
        )
        shapes = [square] + [(rest.shape[0] - 1, *square)] * (rest.shape[0] > 1)
        first, *others = local_call(
            project_node_kernel, [rest, partner_rest, q_own, q_partner], shapes
        )
        rest = others[0] if others else None
    out_rows = 4 * rank // size_rows
    top_rows = lax.dynamic_slice_in_dim(transfer, row * out_rows % rank, out_rows, 1).T
    return (bases, top_rows)


def solution(mesh):
    placed = (P("row", None, None, None), P("row", None), P("row", "col"), P())
    return jax.shard_map(
        shards,
        mesh=mesh,
        in_specs=placed,
        out_specs=(P("row", None), P("row", None)),
        check_vma=False,
    )
```

```python
import functools
import math

import jax
import jax.numpy as jnp
from jax import lax
from jax.experimental import pallas as pl
from jax.experimental.pallas import tpu as pltpu
from jax.sharding import PartitionSpec as P

PANEL = 32
BUSY = 8 * 10**9
NT = (((1,), (1,)), ((), ()))
TN = (((0,), (0,)), ((), ()))


def swap(value, axis, mask):
    pairs = [(source, source ^ mask) for source in range(lax.axis_size(axis))]
    return lax.ppermute(value, axis, pairs)


def split3(value):
    high = value.astype(jnp.bfloat16)
    rest = value - high.astype(jnp.float32)
    mid = rest.astype(jnp.bfloat16)
    low = (rest - mid.astype(jnp.float32)).astype(jnp.bfloat16)
    return high, mid, low


def reciprocal(value):
    guess = pl.reciprocal(value, approx=True)
    return guess * (2.0 - value * guess)


def wide(value, width):
    return jnp.concatenate([value] * (width // value.shape[1]), axis=1)


def eliminate_panel(panel, start):
    rows, width = panel.shape
    tiles = [panel[8 * i : 8 * i + 8, :] for i in range(rows // 8)]
    lanes = lax.broadcasted_iota(jnp.int32, (8, width), 1)
    row_ids = lax.broadcasted_iota(jnp.int32, (8, width), 0)
    for k in range(len(tiles)):
        base = start + 8 * k
        inside = (lanes >= base) & (lanes < base + 8)
        unit = jnp.where(lanes == base + row_ids, 1.0, 0.0)

        def columns(tile):
            return [
                jnp.broadcast_to(tile[:, base + t : base + t + 1], (8, 128)) for t in range(8)
            ]

        below = {i: columns(tiles[i]) for i in range(k + 1, len(tiles))}
        own = columns(tiles[k])
        values = [
            [jnp.broadcast_to(own[u][t : t + 1, :], (8, 128)) if u >= t else None for u in range(8)]
            for t in range(8)
        ]
        top = jnp.where(inside, unit, tiles[k])
        lines = [jnp.broadcast_to(top[t : t + 1, :], (8, width)) for t in range(8)]
        inverses, new = [], None
        for t in range(8):
            inverse = reciprocal(values[t][t])
            inverses.append(inverse)
            for u in range(t + 1, 8):
                ratio = values[t][u] * inverse
                for v in range(u, 8):
                    values[u][v] = values[u][v] - ratio * values[t][v]
                lines[u] = lines[u] - wide(ratio, width) * lines[t]
            scaled = lines[t] * wide(lax.rsqrt(values[t][t]), width)
            new = scaled if new is None else jnp.where(row_ids == t, scaled, new)
        for i in range(len(tiles)):
            if i == k:
                tiles[i] = new
                continue
            tile = jnp.where(inside, 0.0, tiles[i])
            if i > k:
                cols = below[i]
                for t in range(8):
                    factor = cols[t] * inverses[t]
                    for u in range(t + 1, 8):
                        cols[u] = cols[u] - factor * values[t][u]
                    tile = tile - wide(factor, width) * lines[t]
            tiles[i] = tile
    return jnp.concatenate(tiles, axis=0)


def invert_factor(work_ref):
    rank = work_ref.shape[0]
    for start in range(0, rank, PANEL):
        end = start + PANEL
        panel = eliminate_panel(work_ref[start:end, :], start)
        work_ref[start:end, :] = panel
        if end < rank:
            high, mid, low = split3(panel)
            left = jnp.concatenate([high, high, mid, high, low, mid], axis=0)
            right = jnp.concatenate([high, mid, high, low, high, mid], axis=0)
            first = end // 128 * 128
            update = lax.dot_general(
                left[:, first:], right, TN, preferred_element_type=jnp.float32
            )
            later = work_ref[end:, :]
            lanes = lax.broadcasted_iota(jnp.int32, later.shape, 1)
            done = (lanes >= start) & (lanes < end)
            work_ref[end:, :] = jnp.where(done, 0.0, later) - update[end - first :, :]
    shape = (rank, rank)
    lower = lax.broadcasted_iota(jnp.int32, shape, 1) <= lax.broadcasted_iota(jnp.int32, shape, 0)
    return split3(jnp.where(lower, work_ref[...], 0.0))


def gram(value):
    return lax.dot_general(value, value, NT, preferred_element_type=jnp.float32)


def apply_inverse(parts, value, count):
    total = None
    for part in reversed(parts):
        term = jnp.dot(part, value, preferred_element_type=jnp.float32)
        total = term if total is None else total + term
    return (total * math.sqrt(count)).astype(jnp.bfloat16)


def leaf_kernel(col_ref, *refs):
    pieces, (basis_ref, rows_ref, samples_ref, work_ref) = refs[:-4], refs[-4:]
    chunk, count = pieces[0].shape
    for mask, piece in enumerate(pieces):
        place = pl.multiple_of((col_ref[0] ^ mask) * chunk, chunk)
        samples_ref[pl.ds(place, chunk), :] = piece[...]
    work_ref[...] = gram(samples_ref[...])
    parts = invert_factor(work_ref)
    basis = apply_inverse(parts, samples_ref[...], count)
    basis_ref[...] = basis
    rows_ref[...] = basis.T


def node_kernel(own_ref, partner_ref, *refs):
    outs, work_ref = refs[:-1], refs[-1]
    count = 2 * own_ref.shape[1]
    work_ref[...] = gram(own_ref[...]) + gram(partner_ref[...])
    parts = invert_factor(work_ref)
    for source, out in zip((own_ref, partner_ref), outs):
        out[...] = apply_inverse(parts, source[...], count)


def project_leaf_kernel(col_ref, basis_ref, *refs):
    pieces, (first_ref, rest_ref) = refs[:-2], refs[-2:]
    levels, chunk, count = pieces[0].shape
    for mask, piece in enumerate(pieces):
        place = pl.ds(pl.multiple_of((col_ref[0] ^ mask) * chunk, chunk), chunk)
        for level in range(levels):
            moved = lax.dot_general(
                piece[level], basis_ref[...], NT, preferred_element_type=jnp.float32
            )
            moved = (moved * (1.0 / math.sqrt(count))).astype(jnp.bfloat16)
            if level:
                rest_ref[level - 1, place, :] = moved
            else:
                first_ref[place, :] = moved


def project_node_kernel(own_ref, partner_ref, q_own_ref, q_partner_ref, first_ref, *rest):
    count = 2 * own_ref.shape[2]
    for level in range(own_ref.shape[0]):
        moved = lax.dot_general(
            own_ref[level], q_own_ref[...], NT, preferred_element_type=jnp.float32
        ) + lax.dot_general(
            partner_ref[level], q_partner_ref[...], NT, preferred_element_type=jnp.float32
        )
        moved = (moved * (1.0 / math.sqrt(count))).astype(jnp.bfloat16)
        if level:
            rest[0][level - 1] = moved
        else:
            first_ref[...] = moved


def local_call(kernel, args, shapes, scalars=0, scratch=(), flops=0):
    vmem = pl.BlockSpec(memory_space=pltpu.VMEM)
    smem = pl.BlockSpec(memory_space=pltpu.SMEM)
    return pl.pallas_call(
        kernel,
        out_shape=[jax.ShapeDtypeStruct(shape, jnp.bfloat16) for shape in shapes],
        in_specs=[smem] * scalars + [vmem] * (len(args) - scalars),
        out_specs=[vmem] * len(shapes),
        scratch_shapes=list(scratch),
        cost_estimate=pl.CostEstimate(flops=flops, bytes_accessed=2**20, transcendentals=0),
        compiler_params=pltpu.CompilerParams(vmem_limit_bytes=32 * 2**20),
    )(*args)


def products_kernel(source_ref, depth_ref, blocks_ref, sketched_ref, first_ref, rest_ref):
    leaf = pl.program_id(0)
    slots = blocks_ref.shape[1]
    levels = rest_ref.shape[1] + 1
    sums = [jnp.zeros(first_ref.shape[1:], jnp.float32) for _ in range(levels)]
    for slot in range(slots):
        product = lax.dot_general(
            sketched_ref[source_ref[leaf, slot]], blocks_ref[0, slot], NT,
            preferred_element_type=jnp.float32,
        )
        depth = depth_ref[leaf, slot]
        for level in range(levels):
            sums[level] = sums[level] + jnp.where(depth > level, product, 0.0)
    first_ref[0] = sums[0].astype(jnp.bfloat16)
    for level in range(1, levels):
        rest_ref[0, level - 1] = sums[level].astype(jnp.bfloat16)


def off_products(front_blocks, sketched, source, depth, levels):
    leaf_dev, slots, size, _ = front_blocks.shape
    ranks = sketched.shape[1]
    grid_spec = pltpu.PrefetchScalarGridSpec(
        num_scalar_prefetch=2,
        grid=(leaf_dev,),
        in_specs=[
            pl.BlockSpec((1, slots, size, size), lambda i, *_: (i, 0, 0, 0)),
            pl.BlockSpec(sketched.shape, lambda i, *_: (0, 0, 0)),
        ],
        out_specs=[
            pl.BlockSpec((1, ranks, size), lambda i, *_: (i, 0, 0)),
            pl.BlockSpec((1, levels - 1, ranks, size), lambda i, *_: (i, 0, 0, 0)),
        ],
    )
    return pl.pallas_call(
        products_kernel,
        grid_spec=grid_spec,
        out_shape=[
            jax.ShapeDtypeStruct((leaf_dev, ranks, size), jnp.bfloat16),
            jax.ShapeDtypeStruct((leaf_dev, levels - 1, ranks, size), jnp.bfloat16),
        ],
        compiler_params=pltpu.CompilerParams(vmem_limit_bytes=40 * 2**20),
    )(source, depth, front_blocks, sketched)


def front_kernel(sketch_ref, samples_ref, held_ref, part_ref, got_ref, *sems):
    sum_send, sum_recv, chain_send, gather_recv = sems
    row, col = lax.axis_index("row"), lax.axis_index("col")
    size_cols = got_ref.shape[0] + 1
    size_z = held_ref.shape[0] // 2
    leaf_dev, _, cols_dev = samples_ref.shape
    chunk = held_ref.shape[2]
    z = row // 2
    below, above = z > 0, z < size_z - 1

    def signal(where):
        pl.semaphore_signal(
            barrier, inc=1, device_id=where, device_id_type=pl.DeviceIdType.MESH
        )

    barrier = pltpu.get_barrier_semaphore()
    for mask in range(1, size_cols):
        signal({"col": col ^ mask})
    signal({"row": row ^ 1})

    @pl.when(below)
    def _():
        signal({"row": row - 2})

    @pl.when(above)
    def _():
        signal({"row": row + 2})

    pl.semaphore_wait(barrier, size_cols + below.astype(jnp.int32) + above.astype(jnp.int32))

    def sum_copy(mask, leaf):
        peer = col ^ mask
        return pltpu.make_async_remote_copy(
            src_ref=part_ref.at[leaf, pl.ds(pl.multiple_of(peer * chunk, chunk), chunk)],
            dst_ref=got_ref.at[mask - 1, leaf],
            send_sem=sum_send.at[mask - 1, leaf],
            recv_sem=sum_recv.at[mask - 1, leaf],
            device_id={"col": peer},
            device_id_type=pl.DeviceIdType.MESH,
        )

    def gather_copy(way, slot, source, leaf, where):
        return pltpu.make_async_remote_copy(
            src_ref=held_ref.at[source, leaf],
            dst_ref=held_ref.at[source, leaf],
            send_sem=chain_send.at[way, slot, leaf],
            recv_sem=gather_recv.at[source, leaf],
            device_id={"row": where},
            device_id_type=pl.DeviceIdType.MESH,
        )

    def up(distance, leaf):
        return gather_copy(0, distance, row - 2 * distance, leaf, row + 2)

    def down(distance, leaf):
        return gather_copy(1, distance, row + 2 * distance, leaf, row - 2)

    def across(offset, leaf):
        return gather_copy(2, offset % size_z, row + 2 * offset, leaf, row ^ 1)

    matrix = sketch_ref[pl.ds(pl.multiple_of(col * cols_dev, cols_dev), cols_dev), :].T
    for leaf in range(leaf_dev):
        part_ref[leaf] = lax.dot_general(
            matrix, samples_ref[leaf], NT, preferred_element_type=jnp.float32
        ).astype(jnp.bfloat16)
        for mask in range(1, size_cols):
            sum_copy(mask, leaf).start()

    own = pl.ds(pl.multiple_of(col * chunk, chunk), chunk)
    for leaf in range(leaf_dev):
        total = part_ref[leaf, own].astype(jnp.float32)
        for mask in range(1, size_cols):
            sum_copy(mask, leaf).wait_recv()
            total = total + got_ref[mask - 1, leaf].astype(jnp.float32)
        held_ref[row, leaf] = total.astype(jnp.bfloat16)
        pl.when(above)(lambda: up(0, leaf).start())
        pl.when(below)(lambda: down(0, leaf).start())
        across(0, leaf).start()

    for distance in range(1, size_z):
        for leaf in range(leaf_dev):

            @pl.when(z >= distance)
            def _():
                up(distance, leaf).wait_recv()
                pl.when(above)(lambda: up(distance, leaf).start())
                across(-distance, leaf).start()

            @pl.when(z + distance < size_z)
            def _():
                down(distance, leaf).wait_recv()
                pl.when(below)(lambda: down(distance, leaf).start())
                across(distance, leaf).start()

    for leaf in range(leaf_dev):
        for mask in range(1, size_cols):
            sum_copy(mask, leaf).wait_send()
        for other in range(size_z):
            gather_copy(2, 0, 2 * other + 1 - row % 2, leaf, row ^ 1).wait_recv()
        pl.when(above)(lambda: up(0, leaf).wait_send())
        pl.when(below)(lambda: down(0, leaf).wait_send())
        across(0, leaf).wait_send()
        for distance in range(1, size_z):

            @pl.when(z >= distance)
            def _():
                pl.when(above)(lambda: up(distance, leaf).wait_send())
                across(-distance, leaf).wait_send()

            @pl.when(z + distance < size_z)
            def _():
                pl.when(below)(lambda: down(distance, leaf).wait_send())
                across(distance, leaf).wait_send()


def gathered_sketch(sketch_matrix, samples, size_rows, size_cols):
    leaf_dev, size, _ = samples.shape
    rank = sketch_matrix.shape[1]
    chunk = rank // size_cols
    vmem = pl.BlockSpec(memory_space=pltpu.VMEM)
    return pl.pallas_call(
        front_kernel,
        out_shape=jax.ShapeDtypeStruct((size_rows, leaf_dev, chunk, size), jnp.bfloat16),
        in_specs=[vmem, vmem],
        out_specs=vmem,
        scratch_shapes=[
            pltpu.VMEM((leaf_dev, rank, size), jnp.bfloat16),
            pltpu.VMEM((size_cols - 1, leaf_dev, chunk, size), jnp.bfloat16),
            pltpu.SemaphoreType.DMA((size_cols - 1, leaf_dev)),
            pltpu.SemaphoreType.DMA((size_cols - 1, leaf_dev)),
            pltpu.SemaphoreType.DMA((3, size_rows // 2, leaf_dev)),
            pltpu.SemaphoreType.DMA((size_rows, leaf_dev)),
        ],
        compiler_params=pltpu.CompilerParams(
            collective_id=0, has_side_effects=True, vmem_limit_bytes=32 * 2**20
        ),
    )(sketch_matrix, samples)


def shards(front_blocks, block_cols, samples, sketch_matrix):
    leaf_dev, _, leaf_size, _ = front_blocks.shape
    rank = sketch_matrix.shape[1]
    cols_dev = samples.shape[1]
    size_rows, size_cols = lax.axis_size("row"), lax.axis_size("col")
    row, col = lax.axis_index("row"), lax.axis_index("col")
    leaf_total = leaf_dev * size_rows
    top_level = leaf_total.bit_length() - 1
    local_levels = leaf_dev.bit_length() - 1
    held = gathered_sketch(
        sketch_matrix, samples.reshape(leaf_dev, leaf_size, cols_dev), size_rows, size_cols
    ).reshape(leaf_total, rank // size_cols, leaf_size)
    leaf_ids = row * leaf_dev + jnp.arange(leaf_dev, dtype=jnp.int32)
    apart = jnp.bitwise_xor(leaf_ids[:, None], block_cols)
    depth = sum((apart >> level > 0).astype(jnp.int32) for level in range(top_level))
    off_first, off_rest = off_products(front_blocks, held, block_cols, depth, top_level)

    def leaf_of(off, mask):
        return lax.dynamic_index_in_dim(off, (col ^ mask) % leaf_dev, 0, keepdims=False)

    masks = range(1, size_cols)
    here = col.astype(jnp.int32).reshape(1)
    pieces = [leaf_of(off_first, 0)] + [swap(leaf_of(off_first, m), "col", m) for m in masks]
    pieces, off_rest = lax.optimization_barrier((pieces, off_rest))
    later = [leaf_of(off_rest, 0)] + [swap(leaf_of(off_rest, m), "col", m) for m in masks]
    work = pltpu.VMEM((rank, rank), jnp.float32)
    basis, basis_rows = local_call(
        leaf_kernel, [here, *pieces], [(rank, leaf_size), (leaf_size, rank)], 1,
        [pltpu.VMEM((rank, leaf_size), jnp.bfloat16), work], BUSY,
    )
    first, rest = local_call(
        project_leaf_kernel, [here, basis, *later],
        [(rank, rank), (top_level - 2, rank, rank)], 1,
    )

    square = (rank, rank)
    bases = None
    for tree_level in range(1, top_level):
        bit = tree_level - 1
        axis = "col" if bit < local_levels else "row"
        mask = 2 ** (bit if axis == "col" else bit - local_levels)
        partner = swap(first, axis, mask)
        if tree_level == top_level - 1:
            (transfer,) = local_call(node_kernel, [first, partner], [square], 0, [work], BUSY)
            break
        partner, rest = lax.optimization_barrier((partner, rest))
        partner_rest = swap(rest, axis, mask)
        if axis == "row" and bases is None:
            partner, basis_rows = lax.optimization_barrier((partner, basis_rows))
            bases = [basis_rows] + [swap(basis_rows, "col", m) for m in range(1, leaf_dev)]
            order = jnp.arange(leaf_dev, dtype=jnp.int32) ^ (col % leaf_dev)
            bases = jnp.stack(bases)[order].reshape(leaf_dev * leaf_size, rank)
        q_own, q_partner = local_call(
            node_kernel, [first, partner], [square, square], 0, [work], BUSY
        )
        shapes = [square] + [(rest.shape[0] - 1, *square)] * (rest.shape[0] > 1)
        first, *others = local_call(
            project_node_kernel, [rest, partner_rest, q_own, q_partner], shapes
        )
        rest = others[0] if others else None
    out_rows = 4 * rank // size_rows
    top_rows = lax.dynamic_slice_in_dim(transfer, row * out_rows % rank, out_rows, 1).T
    return (bases, top_rows)


def solution(mesh):
    placed = (P("row", None, None, None), P("row", None), P("row", "col"), P())
    return jax.shard_map(
        shards,
        mesh=mesh,
        in_specs=placed,
        out_specs=(P("row", None), P("row", None)),
        check_vma=False,
    )
```

```python
import functools
import math

import jax
import jax.numpy as jnp
from jax import lax
from jax.experimental import pallas as pl
from jax.experimental.pallas import tpu as pltpu
from jax.sharding import PartitionSpec as P

PANEL = 32
BUSY = 8 * 10**9
NT = (((1,), (1,)), ((), ()))
TN = (((0,), (0,)), ((), ()))


def swap(value, axis, mask):
    pairs = [(source, source ^ mask) for source in range(lax.axis_size(axis))]
    return lax.ppermute(value, axis, pairs)


def split3(value):
    high = value.astype(jnp.bfloat16)
    rest = value - high.astype(jnp.float32)
    mid = rest.astype(jnp.bfloat16)
    low = (rest - mid.astype(jnp.float32)).astype(jnp.bfloat16)
    return high, mid, low


def reciprocal(value):
    guess = pl.reciprocal(value, approx=True)
    return guess * (2.0 - value * guess)


def wide(value, width):
    return jnp.concatenate([value] * (width // value.shape[1]), axis=1)


def eliminate_panel(panel, start):
    rows, width = panel.shape
    tiles = [panel[8 * i : 8 * i + 8, :] for i in range(rows // 8)]
    lanes = lax.broadcasted_iota(jnp.int32, (8, width), 1)
    row_ids = lax.broadcasted_iota(jnp.int32, (8, width), 0)
    for k in range(len(tiles)):
        base = start + 8 * k
        inside = (lanes >= base) & (lanes < base + 8)
        unit = jnp.where(lanes == base + row_ids, 1.0, 0.0)

        def columns(tile):
            return [
                jnp.broadcast_to(tile[:, base + t : base + t + 1], (8, 128)) for t in range(8)
            ]

        below = {i: columns(tiles[i]) for i in range(k + 1, len(tiles))}
        own = columns(tiles[k])
        values = [
            [jnp.broadcast_to(own[u][t : t + 1, :], (8, 128)) if u >= t else None for u in range(8)]
            for t in range(8)
        ]
        top = jnp.where(inside, unit, tiles[k])
        lines = [jnp.broadcast_to(top[t : t + 1, :], (8, width)) for t in range(8)]
        inverses, new = [], None
        for t in range(8):
            inverse = reciprocal(values[t][t])
            inverses.append(inverse)
            for u in range(t + 1, 8):
                ratio = values[t][u] * inverse
                for v in range(u, 8):
                    values[u][v] = values[u][v] - ratio * values[t][v]
                lines[u] = lines[u] - wide(ratio, width) * lines[t]
            scaled = lines[t] * wide(lax.rsqrt(values[t][t]), width)
            new = scaled if new is None else jnp.where(row_ids == t, scaled, new)
        for i in range(len(tiles)):
            if i == k:
                tiles[i] = new
                continue
            tile = jnp.where(inside, 0.0, tiles[i])
            if i > k:
                cols = below[i]
                for t in range(8):
                    factor = cols[t] * inverses[t]
                    for u in range(t + 1, 8):
                        cols[u] = cols[u] - factor * values[t][u]
                    tile = tile - wide(factor, width) * lines[t]
            tiles[i] = tile
    return jnp.concatenate(tiles, axis=0)


def invert_factor(work_ref):
    rank = work_ref.shape[0]
    for start in range(0, rank, PANEL):
        end = start + PANEL
        panel = eliminate_panel(work_ref[start:end, :], start)
        work_ref[start:end, :] = panel
        if end < rank:
            high, mid, low = split3(panel)
            left = jnp.concatenate([high, high, mid, high, low, mid], axis=0)
            right = jnp.concatenate([high, mid, high, low, high, mid], axis=0)
            first = end // 128 * 128
            update = lax.dot_general(
                left[:, first:], right, TN, preferred_element_type=jnp.float32
            )
            later = work_ref[end:, :]
            lanes = lax.broadcasted_iota(jnp.int32, later.shape, 1)
            done = (lanes >= start) & (lanes < end)
            work_ref[end:, :] = jnp.where(done, 0.0, later) - update[end - first :, :]
    shape = (rank, rank)
    lower = lax.broadcasted_iota(jnp.int32, shape, 1) <= lax.broadcasted_iota(jnp.int32, shape, 0)
    return split3(jnp.where(lower, work_ref[...], 0.0))


def gram(value):
    return lax.dot_general(value, value, NT, preferred_element_type=jnp.float32)


def apply_inverse(parts, value, count):
    total = None
    for part in reversed(parts):
        term = jnp.dot(part, value, preferred_element_type=jnp.float32)
        total = term if total is None else total + term
    return (total * math.sqrt(count)).astype(jnp.bfloat16)


def leaf_kernel(col_ref, *refs):
    pieces, (basis_ref, rows_ref, samples_ref, work_ref) = refs[:-4], refs[-4:]
    chunk, count = pieces[0].shape
    for mask, piece in enumerate(pieces):
        place = pl.multiple_of((col_ref[0] ^ mask) * chunk, chunk)
        samples_ref[pl.ds(place, chunk), :] = piece[...]
    work_ref[...] = gram(samples_ref[...])
    parts = invert_factor(work_ref)
    basis = apply_inverse(parts, samples_ref[...], count)
    basis_ref[...] = basis
    rows_ref[...] = basis.T


def node_kernel(own_ref, partner_ref, *refs):
    outs, work_ref = refs[:-1], refs[-1]
    count = 2 * own_ref.shape[1]
    work_ref[...] = gram(own_ref[...]) + gram(partner_ref[...])
    parts = invert_factor(work_ref)
    for source, out in zip((own_ref, partner_ref), outs):
        out[...] = apply_inverse(parts, source[...], count)


def project_leaf_kernel(col_ref, basis_ref, *refs):
    pieces, (first_ref, rest_ref) = refs[:-2], refs[-2:]
    levels, chunk, count = pieces[0].shape
    for mask, piece in enumerate(pieces):
        place = pl.ds(pl.multiple_of((col_ref[0] ^ mask) * chunk, chunk), chunk)
        for level in range(levels):
            moved = lax.dot_general(
                piece[level], basis_ref[...], NT, preferred_element_type=jnp.float32
            )
            moved = (moved * (1.0 / math.sqrt(count))).astype(jnp.bfloat16)
            if level:
                rest_ref[level - 1, place, :] = moved
            else:
                first_ref[place, :] = moved


def project_node_kernel(own_ref, partner_ref, q_own_ref, q_partner_ref, first_ref, *rest):
    count = 2 * own_ref.shape[2]
    for level in range(own_ref.shape[0]):
        moved = lax.dot_general(
            own_ref[level], q_own_ref[...], NT, preferred_element_type=jnp.float32
        ) + lax.dot_general(
            partner_ref[level], q_partner_ref[...], NT, preferred_element_type=jnp.float32
        )
        moved = (moved * (1.0 / math.sqrt(count))).astype(jnp.bfloat16)
        if level:
            rest[0][level - 1] = moved
        else:
            first_ref[...] = moved


def local_call(kernel, args, shapes, scalars=0, scratch=(), flops=0):
    vmem = pl.BlockSpec(memory_space=pltpu.VMEM)
    smem = pl.BlockSpec(memory_space=pltpu.SMEM)
    return pl.pallas_call(
        kernel,
        out_shape=[jax.ShapeDtypeStruct(shape, jnp.bfloat16) for shape in shapes],
        in_specs=[smem] * scalars + [vmem] * (len(args) - scalars),
        out_specs=[vmem] * len(shapes),
        scratch_shapes=list(scratch),
        cost_estimate=pl.CostEstimate(flops=flops, bytes_accessed=2**20, transcendentals=0),
        compiler_params=pltpu.CompilerParams(vmem_limit_bytes=32 * 2**20),
    )(*args)


def products_kernel(source_ref, depth_ref, blocks_ref, sketched_ref, first_ref, rest_ref):
    leaf = pl.program_id(0)
    slots = blocks_ref.shape[1]
    levels = rest_ref.shape[1] + 1
    sums = [jnp.zeros(first_ref.shape[1:], jnp.float32) for _ in range(levels)]
    for slot in range(slots):
        product = lax.dot_general(
            sketched_ref[source_ref[leaf, slot]], blocks_ref[0, slot], NT,
            preferred_element_type=jnp.float32,
        )
        depth = depth_ref[leaf, slot]
        for level in range(levels):
            sums[level] = sums[level] + jnp.where(depth > level, product, 0.0)
    first_ref[0] = sums[0].astype(jnp.bfloat16)
    for level in range(1, levels):
        rest_ref[0, level - 1] = sums[level].astype(jnp.bfloat16)


def off_products(front_blocks, sketched, source, depth, levels):
    leaf_dev, slots, size, _ = front_blocks.shape
    ranks = sketched.shape[1]
    grid_spec = pltpu.PrefetchScalarGridSpec(
        num_scalar_prefetch=2,
        grid=(leaf_dev,),
        in_specs=[
            pl.BlockSpec((1, slots, size, size), lambda i, *_: (i, 0, 0, 0)),
            pl.BlockSpec(sketched.shape, lambda i, *_: (0, 0, 0)),
        ],
        out_specs=[
            pl.BlockSpec((1, ranks, size), lambda i, *_: (i, 0, 0)),
            pl.BlockSpec((1, levels - 1, ranks, size), lambda i, *_: (i, 0, 0, 0)),
        ],
    )
    return pl.pallas_call(
        products_kernel,
        grid_spec=grid_spec,
        out_shape=[
            jax.ShapeDtypeStruct((leaf_dev, ranks, size), jnp.bfloat16),
            jax.ShapeDtypeStruct((leaf_dev, levels - 1, ranks, size), jnp.bfloat16),
        ],
        compiler_params=pltpu.CompilerParams(vmem_limit_bytes=24 * 2**20),
    )(source, depth, front_blocks, sketched)


def front_kernel(sketch_ref, samples_ref, held_ref, part_ref, got_ref, *sems):
    sum_send, sum_recv, chain_send, gather_recv = sems
    row, col = lax.axis_index("row"), lax.axis_index("col")
    size_cols = got_ref.shape[0] + 1
    size_z = held_ref.shape[0] // 2
    leaf_dev, _, cols_dev = samples_ref.shape
    chunk = held_ref.shape[2]
    z = row // 2
    below, above = z > 0, z < size_z - 1

    def signal(where):
        pl.semaphore_signal(
            barrier, inc=1, device_id=where, device_id_type=pl.DeviceIdType.MESH
        )

    barrier = pltpu.get_barrier_semaphore()
    for mask in range(1, size_cols):
        signal({"col": col ^ mask})
    signal({"row": row ^ 1})

    @pl.when(below)
    def _():
        signal({"row": row - 2})

    @pl.when(above)
    def _():
        signal({"row": row + 2})

    pl.semaphore_wait(barrier, size_cols + below.astype(jnp.int32) + above.astype(jnp.int32))

    def sum_copy(mask, leaf):
        peer = col ^ mask
        return pltpu.make_async_remote_copy(
            src_ref=part_ref.at[leaf, pl.ds(pl.multiple_of(peer * chunk, chunk), chunk)],
            dst_ref=got_ref.at[mask - 1, leaf],
            send_sem=sum_send.at[mask - 1, leaf],
            recv_sem=sum_recv.at[mask - 1, leaf],
            device_id={"col": peer},
            device_id_type=pl.DeviceIdType.MESH,
        )

    def gather_copy(way, slot, source, leaf, where):
        return pltpu.make_async_remote_copy(
            src_ref=held_ref.at[source, leaf],
            dst_ref=held_ref.at[source, leaf],
            send_sem=chain_send.at[way, slot, leaf],
            recv_sem=gather_recv.at[source, leaf],
            device_id={"row": where},
            device_id_type=pl.DeviceIdType.MESH,
        )

    def up(distance, leaf):
        return gather_copy(0, distance, row - 2 * distance, leaf, row + 2)

    def down(distance, leaf):
        return gather_copy(1, distance, row + 2 * distance, leaf, row - 2)

    def across(offset, leaf):
        return gather_copy(2, offset % size_z, row + 2 * offset, leaf, row ^ 1)

    matrix = sketch_ref[pl.ds(pl.multiple_of(col * cols_dev, cols_dev), cols_dev), :].T
    for leaf in range(leaf_dev):
        part_ref[leaf] = lax.dot_general(
            matrix, samples_ref[leaf], NT, preferred_element_type=jnp.float32
        ).astype(jnp.bfloat16)
        for mask in range(1, size_cols):
            sum_copy(mask, leaf).start()

    own = pl.ds(pl.multiple_of(col * chunk, chunk), chunk)
    for leaf in range(leaf_dev):
        total = part_ref[leaf, own].astype(jnp.float32)
        for mask in range(1, size_cols):
            sum_copy(mask, leaf).wait_recv()
            total = total + got_ref[mask - 1, leaf].astype(jnp.float32)
        held_ref[row, leaf] = total.astype(jnp.bfloat16)
        pl.when(above)(lambda: up(0, leaf).start())
        pl.when(below)(lambda: down(0, leaf).start())
        across(0, leaf).start()

    for distance in range(1, size_z):
        for leaf in range(leaf_dev):

            @pl.when(z >= distance)
            def _():
                up(distance, leaf).wait_recv()
                pl.when(above)(lambda: up(distance, leaf).start())
                across(-distance, leaf).start()

            @pl.when(z + distance < size_z)
            def _():
                down(distance, leaf).wait_recv()
                pl.when(below)(lambda: down(distance, leaf).start())
                across(distance, leaf).start()

    for leaf in range(leaf_dev):
        for mask in range(1, size_cols):
            sum_copy(mask, leaf).wait_send()
        for other in range(size_z):
            gather_copy(2, 0, 2 * other + 1 - row % 2, leaf, row ^ 1).wait_recv()
        pl.when(above)(lambda: up(0, leaf).wait_send())
        pl.when(below)(lambda: down(0, leaf).wait_send())
        across(0, leaf).wait_send()
        for distance in range(1, size_z):

            @pl.when(z >= distance)
            def _():
                pl.when(above)(lambda: up(distance, leaf).wait_send())
                across(-distance, leaf).wait_send()

            @pl.when(z + distance < size_z)
            def _():
                pl.when(below)(lambda: down(distance, leaf).wait_send())
                across(distance, leaf).wait_send()


def gathered_sketch(sketch_matrix, samples, size_rows, size_cols):
    leaf_dev, size, _ = samples.shape
    rank = sketch_matrix.shape[1]
    chunk = rank // size_cols
    vmem = pl.BlockSpec(memory_space=pltpu.VMEM)
    return pl.pallas_call(
        front_kernel,
        out_shape=jax.ShapeDtypeStruct((size_rows, leaf_dev, chunk, size), jnp.bfloat16),
        in_specs=[vmem, vmem],
        out_specs=vmem,
        scratch_shapes=[
            pltpu.VMEM((leaf_dev, rank, size), jnp.bfloat16),
            pltpu.VMEM((size_cols - 1, leaf_dev, chunk, size), jnp.bfloat16),
            pltpu.SemaphoreType.DMA((size_cols - 1, leaf_dev)),
            pltpu.SemaphoreType.DMA((size_cols - 1, leaf_dev)),
            pltpu.SemaphoreType.DMA((3, size_rows // 2, leaf_dev)),
            pltpu.SemaphoreType.DMA((size_rows, leaf_dev)),
        ],
        compiler_params=pltpu.CompilerParams(
            collective_id=0, has_side_effects=True, vmem_limit_bytes=12 * 2**20
        ),
    )(sketch_matrix, samples)


def shards(front_blocks, block_cols, samples, sketch_matrix):
    leaf_dev, _, leaf_size, _ = front_blocks.shape
    rank = sketch_matrix.shape[1]
    cols_dev = samples.shape[1]
    size_rows, size_cols = lax.axis_size("row"), lax.axis_size("col")
    row, col = lax.axis_index("row"), lax.axis_index("col")
    leaf_total = leaf_dev * size_rows
    top_level = leaf_total.bit_length() - 1
    local_levels = leaf_dev.bit_length() - 1
    held = gathered_sketch(
        sketch_matrix, samples.reshape(leaf_dev, leaf_size, cols_dev), size_rows, size_cols
    ).reshape(leaf_total, rank // size_cols, leaf_size)
    leaf_ids = row * leaf_dev + jnp.arange(leaf_dev, dtype=jnp.int32)
    apart = jnp.bitwise_xor(leaf_ids[:, None], block_cols)
    depth = sum((apart >> level > 0).astype(jnp.int32) for level in range(top_level))
    off_first, off_rest = off_products(front_blocks, held, block_cols, depth, top_level)

    def leaf_of(off, mask):
        return lax.dynamic_index_in_dim(off, (col ^ mask) % leaf_dev, 0, keepdims=False)

    masks = range(1, size_cols)
    here = col.astype(jnp.int32).reshape(1)
    pieces = [leaf_of(off_first, 0)] + [swap(leaf_of(off_first, m), "col", m) for m in masks]
    pieces, off_rest = lax.optimization_barrier((pieces, off_rest))
    later = [leaf_of(off_rest, 0)] + [swap(leaf_of(off_rest, m), "col", m) for m in masks]
    work = pltpu.VMEM((rank, rank), jnp.float32)
    basis, basis_rows = local_call(
        leaf_kernel, [here, *pieces], [(rank, leaf_size), (leaf_size, rank)], 1,
        [pltpu.VMEM((rank, leaf_size), jnp.bfloat16), work], BUSY,
    )
    first, rest = local_call(
        project_leaf_kernel, [here, basis, *later],
        [(rank, rank), (top_level - 2, rank, rank)], 1,
    )

    square = (rank, rank)
    bases = None
    for tree_level in range(1, top_level):
        bit = tree_level - 1
        axis = "col" if bit < local_levels else "row"
        mask = 2 ** (bit if axis == "col" else bit - local_levels)
        partner = swap(first, axis, mask)
        if tree_level == top_level - 1:
            (transfer,) = local_call(node_kernel, [first, partner], [square], 0, [work], BUSY)
            break
        partner, rest = lax.optimization_barrier((partner, rest))
        partner_rest = swap(rest, axis, mask)
        if axis == "row" and bases is None:
            partner, basis_rows = lax.optimization_barrier((partner, basis_rows))
            bases = [basis_rows] + [swap(basis_rows, "col", m) for m in range(1, leaf_dev)]
            order = jnp.arange(leaf_dev, dtype=jnp.int32) ^ (col % leaf_dev)
            bases = jnp.stack(bases)[order].reshape(leaf_dev * leaf_size, rank)
        q_own, q_partner = local_call(
            node_kernel, [first, partner], [square, square], 0, [work], BUSY
        )
        shapes = [square] + [(rest.shape[0] - 1, *square)] * (rest.shape[0] > 1)
        first, *others = local_call(
            project_node_kernel, [rest, partner_rest, q_own, q_partner], shapes
        )
        rest = others[0] if others else None
    out_rows = 4 * rank // size_rows
    top_rows = lax.dynamic_slice_in_dim(transfer, row * out_rows % rank, out_rows, 1).T
    return (bases, top_rows)


def solution(mesh):
    placed = (P("row", None, None, None), P("row", None), P("row", "col"), P())
    return jax.shard_map(
        shards,
        mesh=mesh,
        in_specs=placed,
        out_specs=(P("row", None), P("row", None)),
        check_vma=False,
    )
```
